256 devices in a mesh: dp: 32 (over y, x, core), mp: 8 (over z).
Axes of the slice: x: 4, y: 4, z: 8, core: 2. Of those that a mesh axis runs over, the one named last changes fastest.
Arguments:
- gradient: bfloat16 [96, 1024, 1024], P(None, 'dp', 'mp'), may hold values from -0.19921875 to 0.19921875
- slot_block: int32 [96], replicated, may hold values from 0 to 95, each once
- first_moment: float32 [96, 1024, 1024], P(None, 'dp', 'mp')
- second_moment: float32 [96, 1024, 1024], P(None, 'dp', 'mp'), may hold values from 0.0001 to 0.01
- left_stat: float32 [96, 1024, 1024], P('dp', 'mp')
- right_stat: float32 [96, 1024, 1024], P('dp', 'mp')
- left_root: bfloat16 [96, 1024, 1024], P('dp', 'mp')
- right_root: bfloat16 [96, 1024, 1024], P('dp', 'mp')
Outputs:
- update: bfloat16 [96, 1024, 1024], P(None, 'dp', 'mp')
- left_new: float32 [96, 1024, 1024], P('dp', 'mp')
- right_new: float32 [96, 1024, 1024], P('dp', 'mp')
The draws below stay inside these ranges and needn't reach their ends.
Inputs may be any that keep to these rules, and one draw needn't show every extreme that they name: `slot_block`: every block number appears exactly once.
All inputs are finite; a program needn't handle non-finite values. Where the reference program divides by a largest or mean magnitude, that divisor is 1e-20 or more.
Results may differ from the reference program's by a relative error of at most 0.0061.
Values may be sent and summed in bfloat16 or wider, within the bound.
No kernel may reach another device: no remote copies, remote signals or barrier semaphores. Data moves between devices by JAX's collectives and lax.ppermute only.
A program may use at most 128 MiB of HBM per device.

```python
import math
import jax
import jax.numpy as jnp
from jax import lax

BS = 1024
NBLK = 96


def symmetric_block(raw, diagonal, off_scale):
    mirrored = (raw + jnp.swapaxes(raw, 1, 2)) * 0.5 ** 0.5 * off_scale
    identity = jnp.eye(BS, dtype=jnp.float32)[None, :, :]
    return mirrored * (1.0 - identity) + identity * diagonal[:, None, :]


def loguniform_draw(key, shape, lower, upper):
    return jnp.exp(jax.random.uniform(key, shape, jnp.float32, math.log(lower), math.log(upper)))


def draw_first_moment(key, part):
    key = jax.random.fold_in(key, 1)
    key_base, key_rows, key_cols = jax.random.split(key, 3)
    base = jax.random.normal(key_base, (NBLK, BS, BS), jnp.float32)
    rising = jnp.exp(math.log(3.0) * jnp.arange(BS, dtype=jnp.float32) / (BS - 1))[None, :, None]
    row_scale = loguniform_draw(key_rows, (NBLK, BS, 1), 1.0, 3.0)
    col_scale = loguniform_draw(key_cols, (NBLK, 1, BS), 1.0, 10.0)
    return (0.003 * base * rising * row_scale * col_scale).astype(jnp.float32)


def stat_draw(key, lower, upper, off_scale, dtype):
    key_off, key_diag = jax.random.split(key)
    raw = jax.random.normal(key_off, (NBLK, BS, BS), jnp.float32)
    diagonal = jax.random.uniform(key_diag, (NBLK, BS), jnp.float32, lower, upper)
    return symmetric_block(raw, diagonal, off_scale).astype(dtype)


def draw_left_stat(key, part):
    key = jax.random.fold_in(key, 2)
    return stat_draw(key, 0.5, 2.0, 0.02, jnp.float32)


def draw_right_stat(key, part):
    key = jax.random.fold_in(key, 3)
    return stat_draw(key, 0.5, 2.0, 0.02, jnp.float32)


def draw_left_root(key, part):
    key = jax.random.fold_in(key, 4)
    return stat_draw(key, 0.6, 1.4, 0.02, jnp.bfloat16)


def draw_right_root(key, part):
    key = jax.random.fold_in(key, 5)
    return stat_draw(key, 0.6, 1.4, 0.02, jnp.bfloat16)


def levels(key, dims, cuts, low, high):
    gain = 1.0
    for axis_at, blocks in cuts:
        steps = jax.random.uniform(jax.random.fold_in(jax.random.fold_in(key, 6), axis_at), (blocks,), jnp.float32, low / len(cuts), high / len(cuts))
        gain = gain * jnp.repeat(jnp.exp(steps), dims[axis_at] // blocks).reshape((-1,) + (1,) * (len(dims) - 1 - axis_at))
    return gain


def scatter_about(stream_key, extent, spread, reach, shards=(), kind=jnp.bfloat16):
    gain = levels(stream_key, extent, shards, -0.22, 0.18) if shards else 1.0
    drawn = jax.random.normal(stream_key, extent, jnp.float32) * spread * gain
    return jnp.minimum(jnp.maximum(drawn, -reach), reach).astype(kind)


def setup_inputs(seed: int = 0) -> dict:
    key_list = jax.random.split(jax.random.key(seed), 9)
    return {
        "gradient": scatter_about(key_list[0], (NBLK, BS, BS), 0.03, 0.19921875, ((1, 32), (2, 8))),
        "slot_block": jax.random.permutation(key_list[1], NBLK).astype(jnp.int32),
        "first_moment": draw_first_moment(jax.random.fold_in(key_list[8], 71), 0),
        "second_moment": jnp.clip(jnp.exp(math.log(0.01) - 4.6051702 * jax.random.uniform(key_list[3], (NBLK, BS, BS), jnp.float32) ** levels(key_list[3], (NBLK, BS, BS), ((1, 32), (2, 8)), -0.2, 0.2)), 0.0001, 0.01),
        "left_stat": draw_left_stat(jax.random.fold_in(key_list[8], 71), 0),
        "right_stat": draw_right_stat(jax.random.fold_in(key_list[8], 71), 0),
        "left_root": draw_left_root(jax.random.fold_in(key_list[8], 71), 0),
        "right_root": draw_right_root(jax.random.fold_in(key_list[8], 71), 0),
    }


BETA_ONE = 0.9
BETA_TWO = 0.999
ADAM_EPS = 1e-08
STAT_DECAY = 0.9
CLIP_LIMIT = 1.0
NORM_EPS = 1e-06

def reference(gradient, slot_block, first_moment, second_moment, left_stat, right_stat, left_root, right_root):
    grad_wide = gradient.astype(jnp.float32)
    moment_one = BETA_ONE * first_moment + (1.0 - BETA_ONE) * grad_wide
    moment_two = BETA_TWO * second_moment + (1.0 - BETA_TWO) * grad_wide * grad_wide
    adam = moment_one / (jnp.sqrt(moment_two) + ADAM_EPS)
    adam_sq = lax.optimization_barrier(jnp.sum(adam * adam, axis=(1, 2)))
    blocks = jnp.take(gradient, slot_block, axis=0)

    def per_slot(items):
        block, left_old, right_old, left_inv, right_inv = items
        left_next = STAT_DECAY * left_old + (1.0 - STAT_DECAY) * jnp.dot(block, block.T, preferred_element_type=jnp.float32)
        right_next = STAT_DECAY * right_old + (1.0 - STAT_DECAY) * jnp.dot(block.T, block, preferred_element_type=jnp.float32)
        half_done = jnp.dot(left_inv, block, preferred_element_type=jnp.float32).astype(jnp.bfloat16)
        precond = jnp.dot(half_done, right_inv, preferred_element_type=jnp.float32)
        return (left_next, right_next, precond)
    left_new, right_new, precond = lax.map(per_slot, (blocks, left_stat, right_stat, left_root, right_root))
    pre_sq = lax.optimization_barrier(jnp.sum(precond * precond, axis=(1, 2)))
    adam_slot = jnp.take(adam_sq, slot_block, axis=0)
    graft = precond * (jnp.sqrt(adam_slot) / jnp.sqrt(pre_sq + NORM_EPS))[:, None, None]
    largest = jnp.max(jnp.abs(graft))
    counter = jnp.arange(slot_block.shape[0], dtype=jnp.int32)
    inverse = jnp.zeros(slot_block.shape[0], jnp.int32).at[slot_block].set(counter)
    update = (jnp.take(graft, inverse, axis=0) * jnp.minimum(1.0, CLIP_LIMIT / largest)).astype(jnp.bfloat16)
    return (update, left_new, right_new)
```

```python
import functools

import jax
import jax.numpy as jnp
from jax import lax
from jax.experimental import pallas as pl
from jax.experimental.pallas import tpu as pltpu
from jax.sharding import PartitionSpec as P

BETA_ONE = 0.9
BETA_TWO = 0.999
ADAM_EPS = 1e-08
STAT_DECAY = 0.9
CLIP_LIMIT = 1.0
NORM_EPS = 1e-06
PAD = 16
F32 = jnp.float32
BF16 = jnp.bfloat16
SMEM = pltpu.SMEM


def params():
    return pltpu.CompilerParams(vmem_limit_bytes=60 * 1024 * 1024)


def scalars():
    return pl.BlockSpec(memory_space=SMEM)


def whole(shape):
    return pl.BlockSpec(tuple(shape), lambda g: (0,) * len(shape))


def slot_of(shape):
    return pl.BlockSpec((None,) + tuple(shape[1:]), lambda g: (g,) + (0,) * (len(shape) - 1))


def cost(flops, nbytes):
    return pl.CostEstimate(flops=int(flops), bytes_accessed=int(nbytes), transcendentals=0)


def split_rows(values):
    row = lax.broadcasted_iota(jnp.int32, (PAD, 128), 0)
    tile = jnp.zeros((PAD, 128), F32)
    for k, value in enumerate(values):
        high = value.astype(BF16).astype(F32)
        rest = value - high
        middle = rest.astype(BF16).astype(F32)
        low = rest - middle
        for at, piece in enumerate((high, middle, low)):
            tile = jnp.where(row == 3 * k + at, jnp.broadcast_to(piece, (PAD, 128)), tile)
    return tile.astype(BF16)


def joined(tile, k):
    return tile[3 * k : 3 * k + 1] + tile[3 * k + 1 : 3 * k + 2] + tile[3 * k + 2 : 3 * k + 3]


def prepare_kernel(count, slot_ref, grad_ref, one_ref, two_ref, out_ref):
    rows = grad_ref.shape[1]

    def body(owner, _):
        parts = []
        for i in range(count):
            block = slot_ref[owner * count + i]
            grad = grad_ref[block]
            out_ref[owner, i * rows : (i + 1) * rows, :] = grad
            wide = grad.astype(F32)
            moment_one = BETA_ONE * one_ref[block] + (1.0 - BETA_ONE) * wide
            moment_two = BETA_TWO * two_ref[block] + (1.0 - BETA_TWO) * wide * wide
            adam = moment_one / (jnp.sqrt(moment_two) + ADAM_EPS)
            parts.append(jnp.sum(adam * adam, axis=0, keepdims=True))
        out_ref[owner, count * rows :, :] = split_rows(parts)
        return 0

    lax.fori_loop(0, out_ref.shape[0], body, 0)


def prepare(count, owners, slot_block, gradient, first_moment, second_moment):
    rows = gradient.shape[1]
    return pl.pallas_call(
        functools.partial(prepare_kernel, count),
        out_shape=jax.ShapeDtypeStruct((owners, count * rows + PAD, 128), BF16),
        grid=(1,),
        in_specs=[scalars()] + [whole(gradient.shape)] * 3,
        out_specs=whole((owners, count * rows + PAD, 128)),
        compiler_params=params(),
        cost_estimate=cost(20 * gradient.size, 12 * gradient.size),
        name="prepare",
    )(slot_block, gradient, first_moment, second_moment)


def unpack_kernel(got_ref, ring_ref, adam_ref):
    count, order = ring_ref.shape[:2]
    rows = order // got_ref.shape[0]
    for i in range(count):
        ring_ref[i] = got_ref[:, i * rows : (i + 1) * rows, :].reshape(order, 128)
    at = count * rows
    total = got_ref[0, at:, :].astype(F32)
    for d in range(1, got_ref.shape[0]):
        total = total + got_ref[d, at:, :].astype(F32)
    adam_ref[...] = total


def unpack(count, got):
    order = (got.shape[1] - PAD) // count * got.shape[0]
    shape = (count, order, 128)
    return pl.pallas_call(
        unpack_kernel,
        out_shape=[
            jax.ShapeDtypeStruct(shape, BF16),
            jax.ShapeDtypeStruct((PAD, 128), F32),
        ],
        grid=(1,),
        in_specs=[whole(got.shape)],
        out_specs=[whole(shape), whole((PAD, 128))],
        compiler_params=params(),
        cost_estimate=cost(0, 4 * got.size),
        name="unpack",
    )(got)


class RingPanels:
    def __init__(self, place, refs):
        self.place = place
        self.refs = refs

    def place_of(self, k):
        return lax.rem(self.place + k, 8)

    def rows(self, k, low, high):
        if k != 4:
            return self.refs[k if k < 4 else k + 1][low:high, :]
        upper, lower = self.refs[4:6]
        half = upper.shape[0]
        if high <= half:
            return upper[low:high, :]
        if low >= half:
            return lower[low - half : high - half, :]
        return jnp.concatenate([upper[low:, :], lower[: high - half, :]], axis=0)

    def rows_at(self, k, at):
        if k != 4:
            return self.refs[k if k < 4 else k + 1][pl.ds(at, 128), :]
        upper, lower = self.refs[4:6]
        half = upper.shape[0]
        inside = pl.ds(pl.multiple_of(lax.rem(at, half), 128), 128)
        return jnp.where(at < half, upper[inside, :], lower[inside, :])

    def mine(self):
        return self.refs[0][...]


def pair_of(grads, k, order):
    return jnp.concatenate([grads.rows(2 * k + e, 0, order) for e in range(2)], axis=1)


def precondition_kernel(place_ref, left_ref, adam_ref, *refs):
    out_ref = refs[-1]
    grads, roots = RingPanels(place_ref[0], refs[:9]), refs[9:18]
    order = left_ref.shape[1]
    step = pl.program_id(0)
    base = pl.multiple_of(step * (128 + PAD), PAD)
    left = left_ref[...]
    half = []
    for k in range(4):
        pair = pair_of(grads, k, order)
        half.append(jnp.dot(left, pair, preferred_element_type=F32).astype(BF16))
    half = jnp.concatenate(half, axis=1)
    square = jnp.zeros((1, 128), F32)
    largest = jnp.zeros((1, 128), F32)
    for c in range(4):
        parts = [ref[:, 256 * c : 256 * (c + 1)] for ref in roots]
        pre = jnp.dot(half, jnp.concatenate(parts, axis=0), preferred_element_type=F32)
        for e in range(2):
            piece = pre[:, 128 * e : 128 * (e + 1)]
            out_ref[2 * c + e, pl.ds(base, 128), :] = piece.astype(BF16)
            square = square + jnp.sum(piece * piece, axis=0, keepdims=True)
            largest = jnp.maximum(largest, jnp.max(jnp.abs(piece), axis=0, keepdims=True))
    low = 3 * step
    row = lax.broadcasted_iota(jnp.int32, (PAD, 128), 0)
    inside = (row >= low) & (row < low + 3)
    adam = jnp.sum(jnp.where(inside, adam_ref[...], 0.0), axis=0, keepdims=True)
    tile = split_rows([adam, square, largest])
    tail = pl.multiple_of(base + 128, PAD)
    for k in range(8):
        out_ref[k, pl.ds(tail, PAD), :] = tile


def precondition(place, left_root, adam, grads, roots):
    count, _, order = left_root.shape
    out = (8, count * (128 + PAD), 128)
    return pl.pallas_call(
        precondition_kernel,
        out_shape=jax.ShapeDtypeStruct(out, BF16),
        grid=(count,),
        in_specs=[scalars(), slot_of(left_root.shape), whole(adam.shape)]
        + [slot_of(panel.shape) for panel in (*grads, *roots)],
        out_specs=whole(out),
        compiler_params=params(),
        cost_estimate=cost(count * 4 * 128 * order * order, count * 5 * order * order),
        name="precondition",
    )(place, left_root, adam, *grads, *roots)


def scale_kernel(count, got_ref, out_ref):
    rows = (out_ref.shape[1] - PAD) // count
    step = min(rows, 128)
    scales = []
    peak = jnp.zeros((1, 128), F32)
    for i in range(count):
        base = i * (128 + PAD)
        adam = square = largest = None
        for k in range(8):
            tile = got_ref[k, base + 128 : base + 128 + PAD, :].astype(F32)
            a, s, m = joined(tile, 0), joined(tile, 1), joined(tile, 2)
            adam = a if adam is None else adam + a
            square = s if square is None else square + s
            largest = m if largest is None else jnp.maximum(largest, m)
        adam = jnp.sum(adam, axis=1, keepdims=True)
        square = jnp.sum(square, axis=1, keepdims=True)
        largest = jnp.max(largest, axis=1, keepdims=True)
        scale = jnp.broadcast_to(jnp.sqrt(adam) / jnp.sqrt(square + NORM_EPS), (1, 128))
        scales.append(scale)
        peak = jnp.maximum(peak, scale * jnp.broadcast_to(largest, (1, 128)))
    tile = split_rows(scales + [peak])
    for d in range(out_ref.shape[0]):
        for i in range(count):
            for at in range(0, rows, step):
                row = d * rows + at
                low = i * (128 + PAD) + row % 128
                to = i * rows + at
                out_ref[d, to : to + step, :] = got_ref[row // 128, low : low + step, :]
        out_ref[d, count * rows :, :] = tile


def scale_up(owners, count, order, got):
    out = (owners, count * (order // owners) + PAD, 128)
    return pl.pallas_call(
        functools.partial(scale_kernel, count),
        out_shape=jax.ShapeDtypeStruct(out, BF16),
        grid=(1,),
        in_specs=[whole(got.shape)],
        out_specs=whole(out),
        compiler_params=params(),
        cost_estimate=cost(0, 4 * got.size),
        name="scale",
    )(got)


def finish_kernel(count, slot_ref, got_ref, out_ref):
    rows = out_ref.shape[1]
    owners = got_ref.shape[0]

    def carried(owner, k):
        return joined(got_ref[owner, count * rows :, :].astype(F32), k)

    def find(owner, peak):
        return jnp.maximum(peak, carried(owner, count))

    peak = lax.fori_loop(0, owners, find, jnp.zeros((1, 128), F32))
    clip = jnp.minimum(1.0, CLIP_LIMIT / peak)

    def body(owner, _):
        for i in range(count):
            graft = got_ref[owner, i * rows : (i + 1) * rows, :].astype(F32) * carried(owner, i)
            out_ref[slot_ref[owner * count + i]] = (graft * clip).astype(BF16)
        return 0

    lax.fori_loop(0, owners, body, 0)


def finish(count, slot_block, got):
    out = (slot_block.shape[0], (got.shape[1] - PAD) // count, 128)
    return pl.pallas_call(
        functools.partial(finish_kernel, count),
        out_shape=jax.ShapeDtypeStruct(out, BF16),
        grid=(1,),
        in_specs=[scalars(), whole(got.shape)],
        out_specs=whole(out),
        compiler_params=params(),
        cost_estimate=cost(0, 4 * got.size),
        name="finish",
    )(slot_block, got)


def factors_kernel(place_ref, left_ref, right_ref, *refs):
    left_out, right_out = refs[-2:]
    order = left_ref.shape[1]
    place = place_ref[0]
    grads = RingPanels(place, refs[:9])
    at = pl.multiple_of(place * 128, 128)
    mine = jnp.concatenate([grads.rows_at(k, at) for k in range(8)], axis=1)
    for c in range(4):
        low = 256 * c
        rows = jnp.concatenate([grads.rows(k, low, low + 256) for k in range(8)], axis=1)
        part = lax.dot_general(
            mine, rows, (((1,), (1,)), ((), ())), preferred_element_type=F32
        )
        old = left_ref[:, low : low + 256]
        left_out[:, low : low + 256] = STAT_DECAY * old + (1.0 - STAT_DECAY) * part
    turned = grads.mine().T
    for k in range(4):
        part = jnp.dot(turned, pair_of(grads, k, order), preferred_element_type=F32)
        for e in range(2):
            to = grads.place_of(2 * k + e) * 128
            column = pl.ds(to if isinstance(to, int) else pl.multiple_of(to, 128), 128)
            old = right_ref[:, column]
            new = STAT_DECAY * old + (1.0 - STAT_DECAY) * part[:, 128 * e : 128 * (e + 1)]
            right_out[:, column] = new


def factors(place, left_stat, right_stat, grads):
    count, _, order = left_stat.shape
    return pl.pallas_call(
        factors_kernel,
        out_shape=[jax.ShapeDtypeStruct(left_stat.shape, F32)] * 2,
        grid=(count,),
        in_specs=[scalars(), slot_of(left_stat.shape), slot_of(right_stat.shape)]
        + [slot_of(grad.shape) for grad in grads],
        out_specs=[slot_of(left_stat.shape)] * 2,
        compiler_params=params(),
        cost_estimate=cost(count * 4 * 128 * order * order, count * 4 * order * order),
        name="factors",
    )(place, left_stat, right_stat, *grads)


def ring(own, axis):
    up = [(i, (i + 1) % 8) for i in range(8)]
    down = [(i, (i - 1) % 8) for i in range(8)]
    from_below, from_above = [own], [own]
    for _ in range(3):
        from_below.append(lax.ppermute(from_below[-1], "mp", up))
        from_above.append(lax.ppermute(from_above[-1], "mp", down))
    size = own.shape[axis]
    first = lax.slice_in_dim(from_below[3], 0, size // 2, axis=axis)
    second = lax.slice_in_dim(from_above[3], size // 2, size, axis=axis)
    first = lax.ppermute(first, "mp", up)
    second = lax.ppermute(second, "mp", down)
    return from_above + [first, second] + from_below[:0:-1]


def shards(
    gradient, slot_block, first_moment, second_moment, left_stat, right_stat, left_root, right_root
):
    count, _, order = left_stat.shape
    owners = gradient.shape[0] // count
    place = lax.axis_index("mp").astype(jnp.int32).reshape(1)
    roots = ring(right_root, 1)
    sent = prepare(count, owners, slot_block, gradient, first_moment, second_moment)
    got = lax.all_to_all(sent, "dp", split_axis=0, concat_axis=0, tiled=True)
    own, adam = unpack(count, got)
    own, _ = lax.optimization_barrier((own, (roots[3], roots[6])))
    grads = ring(own, 1)
    sent = precondition(place, left_root, adam, grads, roots)
    got = lax.all_to_all(sent, "mp", split_axis=0, concat_axis=0, tiled=True)
    sent = scale_up(owners, count, order, got)
    got = lax.all_to_all(sent, "dp", split_axis=0, concat_axis=0, tiled=True)
    left_new, right_new = factors(place, left_stat, right_stat, grads)
    update = finish(count, slot_block, got)
    return (update, left_new, right_new)


def solution(mesh):
    return jax.shard_map(
        shards,
        mesh=mesh,
        in_specs=(
            P(None, "dp", "mp"),
            P(),
            P(None, "dp", "mp"),
            P(None, "dp", "mp"),
            P("dp", "mp", None),
            P("dp", "mp", None),
            P("dp", "mp", None),
            P("dp", "mp", None),
        ),
        out_specs=(P(None, "dp", "mp"), P("dp", "mp", None), P("dp", "mp", None)),
        check_vma=False,
    )
```

```python
import functools

import jax
import jax.numpy as jnp
from jax import lax
from jax.experimental import pallas as pl
from jax.experimental.pallas import tpu as pltpu
from jax.sharding import PartitionSpec as P

BETA_ONE = 0.9
BETA_TWO = 0.999
ADAM_EPS = 1e-08
STAT_DECAY = 0.9
CLIP_LIMIT = 1.0
NORM_EPS = 1e-06
PAD = 16
F32 = jnp.float32
BF16 = jnp.bfloat16
SMEM = pltpu.SMEM


def params():
    return pltpu.CompilerParams(vmem_limit_bytes=62 * 1024 * 1024)


def scalars():
    return pl.BlockSpec(memory_space=SMEM)


def whole(shape):
    return pl.BlockSpec(tuple(shape), lambda g: (0,) * len(shape))


def slot_of(shape):
    return pl.BlockSpec((None,) + tuple(shape[1:]), lambda g: (g,) + (0,) * (len(shape) - 1))


def cost(flops, nbytes):
    return pl.CostEstimate(flops=int(flops), bytes_accessed=int(nbytes), transcendentals=0)


def split_rows(values):
    row = lax.broadcasted_iota(jnp.int32, (PAD, 128), 0)
    tile = jnp.zeros((PAD, 128), F32)
    for k, value in enumerate(values):
        high = value.astype(BF16).astype(F32)
        rest = value - high
        middle = rest.astype(BF16).astype(F32)
        low = rest - middle
        for at, piece in enumerate((high, middle, low)):
            tile = jnp.where(row == 3 * k + at, jnp.broadcast_to(piece, (PAD, 128)), tile)
    return tile.astype(BF16)


def joined(tile, k):
    return tile[3 * k : 3 * k + 1] + tile[3 * k + 1 : 3 * k + 2] + tile[3 * k + 2 : 3 * k + 3]


def prepare_kernel(count, slot_ref, grad_ref, one_ref, two_ref, out_ref):
    rows = grad_ref.shape[1]

    def body(owner, _):
        parts = []
        for i in range(count):
            block = slot_ref[owner * count + i]
            grad = grad_ref[block]
            out_ref[owner, i * rows : (i + 1) * rows, :] = grad
            wide = grad.astype(F32)
            moment_one = BETA_ONE * one_ref[block] + (1.0 - BETA_ONE) * wide
            moment_two = BETA_TWO * two_ref[block] + (1.0 - BETA_TWO) * wide * wide
            adam = moment_one / (jnp.sqrt(moment_two) + ADAM_EPS)
            parts.append(jnp.sum(adam * adam, axis=0, keepdims=True))
        out_ref[owner, count * rows :, :] = split_rows(parts)
        return 0

    lax.fori_loop(0, out_ref.shape[0], body, 0)


def prepare(count, owners, slot_block, gradient, first_moment, second_moment):
    rows = gradient.shape[1]
    return pl.pallas_call(
        functools.partial(prepare_kernel, count),
        out_shape=jax.ShapeDtypeStruct((owners, count * rows + PAD, 128), BF16),
        grid=(1,),
        in_specs=[scalars()] + [whole(gradient.shape)] * 3,
        out_specs=whole((owners, count * rows + PAD, 128)),
        compiler_params=params(),
        cost_estimate=cost(20 * gradient.size, 12 * gradient.size),
        name="prepare",
    )(slot_block, gradient, first_moment, second_moment)


def unpack_kernel(got_ref, ring_ref, adam_ref):
    count, order = ring_ref.shape[:2]
    rows = order // got_ref.shape[0]
    for i in range(count):
        ring_ref[i] = got_ref[:, i * rows : (i + 1) * rows, :].reshape(order, 128)
    at = count * rows
    total = got_ref[0, at:, :].astype(F32)
    for d in range(1, got_ref.shape[0]):
        total = total + got_ref[d, at:, :].astype(F32)
    adam_ref[...] = total


def unpack(count, got):
    order = (got.shape[1] - PAD) // count * got.shape[0]
    shape = (count, order, 128)
    return pl.pallas_call(
        unpack_kernel,
        out_shape=[
            jax.ShapeDtypeStruct(shape, BF16),
            jax.ShapeDtypeStruct((PAD, 128), F32),
        ],
        grid=(1,),
        in_specs=[whole(got.shape)],
        out_specs=[whole(shape), whole((PAD, 128))],
        compiler_params=params(),
        cost_estimate=cost(0, 4 * got.size),
        name="unpack",
    )(got)


class RingPanels:
    def __init__(self, place, refs):
        self.place = place
        self.refs = refs

    def place_of(self, k):
        return lax.rem(self.place + k, 8)

    def rows(self, k, low, high):
        if k != 4:
            return self.refs[k if k < 4 else k + 1][low:high, :]
        upper, lower = self.refs[4:6]
        half = upper.shape[0]
        if high <= half:
            return upper[low:high, :]
        if low >= half:
            return lower[low - half : high - half, :]
        return jnp.concatenate([upper[low:, :], lower[: high - half, :]], axis=0)

    def rows_at(self, k, at):
        if k != 4:
            return self.refs[k if k < 4 else k + 1][pl.ds(at, 128), :]
        upper, lower = self.refs[4:6]
        half = upper.shape[0]
        inside = pl.ds(pl.multiple_of(lax.rem(at, half), 128), 128)
        return jnp.where(at < half, upper[inside, :], lower[inside, :])

    def mine(self):
        return self.refs[0][...]


def pair_of(grads, k, order):
    return jnp.concatenate([grads.rows(2 * k + e, 0, order) for e in range(2)], axis=1)


def bulk_kernel(left_ref, *refs):
    grads, roots, out_ref = refs[:7], refs[7:14], refs[14]
    left = left_ref[...]
    half = []
    for k in (0, 2, 4, 6):
        pair = [ref[...] for ref in grads[k : k + 2]]
        pair = jnp.concatenate(pair, axis=1) if len(pair) > 1 else pair[0]
        half.append(jnp.dot(left, pair, preferred_element_type=F32).astype(BF16))
    half = jnp.concatenate(half, axis=1)
    for c in range(4):
        column = slice(256 * c, 256 * (c + 1))
        part = jnp.concatenate([ref[:, column] for ref in roots], axis=0)
        out_ref[:, column] = jnp.dot(half, part, preferred_element_type=F32)


def bulk(left_root, grads, roots):
    count, rows, order = left_root.shape
    early = [*grads[:4], *grads[6:], *roots[:4], *roots[6:]]
    return pl.pallas_call(
        bulk_kernel,
        out_shape=jax.ShapeDtypeStruct(left_root.shape, F32),
        grid=(count,),
        in_specs=[slot_of(left_root.shape)] + [slot_of(panel.shape) for panel in early],
        out_specs=slot_of(left_root.shape),
        compiler_params=params(),
        cost_estimate=cost(count * 4 * rows * order * order, count * 5 * order * order),
        name="bulk",
    )(left_root, *early)


def precondition_kernel(place_ref, left_ref, adam_ref, part_ref, *refs):
    out_refs, sums_ref = refs[4:12], refs[12]
    count = pl.num_programs(0)
    step = pl.program_id(0)
    rows = pl.ds(pl.multiple_of(step * 128, 128), 128)
    panel = jnp.concatenate([refs[0][...], refs[1][...]], axis=0)
    half = jnp.dot(left_ref[...], panel, preferred_element_type=F32).astype(BF16)
    square = jnp.zeros((1, 128), F32)
    largest = jnp.zeros((1, 128), F32)
    for k in range(8):
        column = pl.ds(pl.multiple_of(lax.rem(place_ref[0] + k, 8) * 128, 128), 128)
        root = jnp.concatenate([refs[2][:, column], refs[3][:, column]], axis=0)
        pre = part_ref[:, column] + jnp.dot(half, root, preferred_element_type=F32)
        out_refs[k][rows, :] = pre.astype(BF16)
        square = square + jnp.sum(pre * pre, axis=0, keepdims=True)
        largest = jnp.maximum(largest, jnp.max(jnp.abs(pre), axis=0, keepdims=True))
    low = 3 * step
    row = lax.broadcasted_iota(jnp.int32, (PAD, 128), 0)
    inside = (row >= low) & (row < low + 3)
    adam = jnp.sum(jnp.where(inside, adam_ref[...], 0.0), axis=0, keepdims=True)
    lane = lax.broadcasted_iota(jnp.int32, (1, 128), 1)

    @pl.when(step == 0)
    def _():
        sums_ref[...] = jnp.zeros((1, 128), F32)

    sums = sums_ref[...]
    for at, value in (
        (step, jnp.sum(adam, axis=1, keepdims=True)),
        (count + step, jnp.sum(square, axis=1, keepdims=True)),
        (2 * count + step, jnp.max(largest, axis=1, keepdims=True)),
    ):
        sums = jnp.where(lane == at, jnp.broadcast_to(value, (1, 128)), sums)
    sums_ref[...] = sums

    @pl.when(step == count - 1)
    def _():
        tile = split_rows([sums])
        for out_ref in out_refs:
            out_ref[out_ref.shape[0] - PAD :, :] = tile


def precondition(place, left_root, adam, part, grads, roots):
    count, rows, order = left_root.shape
    out = (count * rows + PAD, 128)
    late = [*grads[4:6], *roots[4:6]]
    return pl.pallas_call(
        precondition_kernel,
        out_shape=[jax.ShapeDtypeStruct(out, BF16)] * 8,
        grid=(count,),
        in_specs=[scalars(), slot_of(left_root.shape), whole(adam.shape), slot_of(part.shape)]
        + [slot_of(panel.shape) for panel in late],
        out_specs=[whole(out)] * 8,
        scratch_shapes=[pltpu.VMEM((1, 128), F32)],
        compiler_params=params(),
        cost_estimate=cost(count * 4 * rows * 128 * order, count * 4 * rows * order),
        name="precondition",
    )(place, left_root, adam, part, *late)


def scale_kernel(count, place_ref, *refs):
    got_refs, out_ref = refs[:-1], refs[-1]
    rows = (out_ref.shape[1] - PAD) // count
    each = 128 // rows
    lane = lax.broadcasted_iota(jnp.int32, (1, 128), 1)
    total = largest = jnp.zeros((1, 128), F32)
    for ref in got_refs:
        values = joined(ref[count * 128 :, :].astype(F32), 0)
        total = total + values
        largest = jnp.maximum(largest, values)

    def only(values, at):
        one = jnp.sum(jnp.where(lane == at, values, 0.0), axis=1, keepdims=True)
        return jnp.broadcast_to(one, (1, 128))

    scales = []
    peak = jnp.zeros((1, 128), F32)
    for i in range(count):
        adam, square = only(total, i), only(total, count + i)
        scale = jnp.sqrt(adam) / jnp.sqrt(square + NORM_EPS)
        scales.append(scale)
        peak = jnp.maximum(peak, scale * only(largest, 2 * count + i))
    tile = split_rows(scales + [peak])
    for k, ref in enumerate(got_refs):
        first = lax.rem(place_ref[0] + 8 - k, 8) * each
        for e in range(each):
            for i in range(count):
                low = i * 128 + e * rows
                out_ref[first + e, i * rows : (i + 1) * rows, :] = ref[low : low + rows, :]
            out_ref[first + e, count * rows :, :] = tile


def scale_up(owners, count, place, gots):
    out = (owners, count * (1024 // owners) + PAD, 128)
    return pl.pallas_call(
        functools.partial(scale_kernel, count),
        out_shape=jax.ShapeDtypeStruct(out, BF16),
        grid=(1,),
        in_specs=[scalars()] + [whole(got.shape) for got in gots],
        out_specs=whole(out),
        compiler_params=params(),
        cost_estimate=cost(0, 32 * gots[0].size),
        name="scale",
    )(place, *gots)


def finish_kernel(count, slot_ref, got_ref, out_ref):
    rows = out_ref.shape[1]
    owners = got_ref.shape[0]

    def carried(owner, k):
        return joined(got_ref[owner, count * rows :, :].astype(F32), k)

    def find(owner, peak):
        return jnp.maximum(peak, carried(owner, count))

    peak = lax.fori_loop(0, owners, find, jnp.zeros((1, 128), F32))
    clip = jnp.minimum(1.0, CLIP_LIMIT / peak)

    def body(owner, _):
        for i in range(count):
            graft = got_ref[owner, i * rows : (i + 1) * rows, :].astype(F32) * carried(owner, i)
            out_ref[slot_ref[owner * count + i]] = (graft * clip).astype(BF16)
        return 0

    lax.fori_loop(0, owners, body, 0)


def finish(count, slot_block, got):
    out = (slot_block.shape[0], (got.shape[1] - PAD) // count, 128)
    return pl.pallas_call(
        functools.partial(finish_kernel, count),
        out_shape=jax.ShapeDtypeStruct(out, BF16),
        grid=(1,),
        in_specs=[scalars(), whole(got.shape)],
        out_specs=whole(out),
        compiler_params=params(),
        cost_estimate=cost(0, 4 * got.size),
        name="finish",
    )(slot_block, got)


def factors_kernel(place_ref, left_ref, right_ref, *refs):
    left_out, right_out = refs[-2:]
    order = left_ref.shape[1]
    place = place_ref[0]
    grads = RingPanels(place, refs[:9])
    at = pl.multiple_of(place * 128, 128)
    mine = jnp.concatenate([grads.rows_at(k, at) for k in range(8)], axis=1)
    for c in range(4):
        low = 256 * c
        rows = jnp.concatenate([grads.rows(k, low, low + 256) for k in range(8)], axis=1)
        part = lax.dot_general(
            mine, rows, (((1,), (1,)), ((), ())), preferred_element_type=F32
        )
        old = left_ref[:, low : low + 256]
        left_out[:, low : low + 256] = STAT_DECAY * old + (1.0 - STAT_DECAY) * part
    turned = grads.mine().T
    for k in range(4):
        part = jnp.dot(turned, pair_of(grads, k, order), preferred_element_type=F32)
        for e in range(2):
            to = grads.place_of(2 * k + e) * 128
            column = pl.ds(to if isinstance(to, int) else pl.multiple_of(to, 128), 128)
            old = right_ref[:, column]
            new = STAT_DECAY * old + (1.0 - STAT_DECAY) * part[:, 128 * e : 128 * (e + 1)]
            right_out[:, column] = new


def factors(place, left_stat, right_stat, grads):
    count, _, order = left_stat.shape
    return pl.pallas_call(
        factors_kernel,
        out_shape=[jax.ShapeDtypeStruct(left_stat.shape, F32)] * 2,
        grid=(count,),
        in_specs=[scalars(), slot_of(left_stat.shape), slot_of(right_stat.shape)]
        + [slot_of(grad.shape) for grad in grads],
        out_specs=[slot_of(left_stat.shape)] * 2,
        compiler_params=params(),
        cost_estimate=cost(count * 4 * 128 * order * order, count * 4 * order * order),
        name="factors",
    )(place, left_stat, right_stat, *grads)


def ring(own, axis):
    up = [(i, (i + 1) % 8) for i in range(8)]
    down = [(i, (i - 1) % 8) for i in range(8)]
    from_below, from_above = [own], [own]
    for _ in range(3):
        from_below.append(lax.ppermute(from_below[-1], "mp", up))
        from_above.append(lax.ppermute(from_above[-1], "mp", down))
    size = own.shape[axis]
    first = lax.slice_in_dim(from_below[3], 0, size // 2, axis=axis)
    second = lax.slice_in_dim(from_above[3], size // 2, size, axis=axis)
    first = lax.ppermute(first, "mp", up)
    second = lax.ppermute(second, "mp", down)
    return from_above + [first, second] + from_below[:0:-1]


def shards(
    gradient, slot_block, first_moment, second_moment, left_stat, right_stat, left_root, right_root
):
    count = left_stat.shape[0]
    owners = gradient.shape[0] // count
    place = lax.axis_index("mp").astype(jnp.int32).reshape(1)
    roots = ring(right_root, 1)
    sent = prepare(count, owners, slot_block, gradient, first_moment, second_moment)
    got = lax.all_to_all(sent, "dp", split_axis=0, concat_axis=0, tiled=True)
    own, adam = unpack(count, got)
    own, _ = lax.optimization_barrier((own, (roots[3], roots[6])))
    grads = ring(own, 1)
    part = bulk(left_root, grads, roots)
    sents = precondition(place, left_root, adam, part, grads, roots)
    gots = list(sents)
    for k in (4, 3, 5, 2, 6, 1, 7):
        gots[k] = lax.ppermute(sents[k], "mp", [(i, (i + k) % 8) for i in range(8)])
    sent = scale_up(owners, count, place, gots)
    got = lax.all_to_all(sent, "dp", split_axis=0, concat_axis=0, tiled=True)
    left_new, right_new = factors(place, left_stat, right_stat, grads)
    update = finish(count, slot_block, got)
    return (update, left_new, right_new)


def solution(mesh):
    return jax.shard_map(
        shards,
        mesh=mesh,
        in_specs=(
            P(None, "dp", "mp"),
            P(),
            P(None, "dp", "mp"),
            P(None, "dp", "mp"),
            P("dp", "mp", None),
            P("dp", "mp", None),
            P("dp", "mp", None),
            P("dp", "mp", None),
        ),
        out_specs=(P(None, "dp", "mp"), P("dp", "mp", None), P("dp", "mp", None)),
        check_vma=False,
    )
```

```python
import functools

import jax
import jax.numpy as jnp
from jax import lax
from jax.experimental import pallas as pl
from jax.experimental.pallas import tpu as pltpu
from jax.sharding import PartitionSpec as P

BETA_ONE = 0.9
BETA_TWO = 0.999
ADAM_EPS = 1e-08
STAT_DECAY = 0.9
CLIP_LIMIT = 1.0
NORM_EPS = 1e-06
PAD = 16
F32 = jnp.float32
BF16 = jnp.bfloat16
SMEM = pltpu.SMEM


def params(mib):
    return pltpu.CompilerParams(vmem_limit_bytes=mib * 1024 * 1024)


def scalars():
    return pl.BlockSpec(memory_space=SMEM)


def whole(shape):
    return pl.BlockSpec(tuple(shape), lambda g: (0,) * len(shape))


def slot_of(shape):
    return pl.BlockSpec((None,) + tuple(shape[1:]), lambda g: (g,) + (0,) * (len(shape) - 1))


def cost(flops, nbytes):
    return pl.CostEstimate(flops=int(flops), bytes_accessed=int(nbytes), transcendentals=0)


def split_rows(values):
    row = lax.broadcasted_iota(jnp.int32, (PAD, 128), 0)
    tile = jnp.zeros((PAD, 128), F32)
    for k, value in enumerate(values):
        high = value.astype(BF16).astype(F32)
        rest = value - high
        middle = rest.astype(BF16).astype(F32)
        low = rest - middle
        for at, piece in enumerate((high, middle, low)):
            tile = jnp.where(row == 3 * k + at, jnp.broadcast_to(piece, (PAD, 128)), tile)
    return tile.astype(BF16)


def joined(tile, k):
    return tile[3 * k : 3 * k + 1] + tile[3 * k + 1 : 3 * k + 2] + tile[3 * k + 2 : 3 * k + 3]


def prepare_kernel(count, slot_ref, grad_ref, one_ref, two_ref, out_ref):
    rows = grad_ref.shape[1]

    def body(owner, _):
        parts = []
        for i in range(count):
            block = slot_ref[owner * count + i]
            grad = grad_ref[block]
            out_ref[owner, i * rows : (i + 1) * rows, :] = grad
            wide = grad.astype(F32)
            moment_one = BETA_ONE * one_ref[block] + (1.0 - BETA_ONE) * wide
            moment_two = BETA_TWO * two_ref[block] + (1.0 - BETA_TWO) * wide * wide
            adam = moment_one / (jnp.sqrt(moment_two) + ADAM_EPS)
            parts.append(jnp.sum(adam * adam, axis=0, keepdims=True))
        out_ref[owner, count * rows :, :] = split_rows(parts)
        return 0

    lax.fori_loop(0, out_ref.shape[0], body, 0)


def prepare(count, owners, slot_block, gradient, first_moment, second_moment):
    rows = gradient.shape[1]
    return pl.pallas_call(
        functools.partial(prepare_kernel, count),
        out_shape=jax.ShapeDtypeStruct((owners, count * rows + PAD, 128), BF16),
        grid=(1,),
        in_specs=[scalars()] + [whole(gradient.shape)] * 3,
        out_specs=whole((owners, count * rows + PAD, 128)),
        compiler_params=params(62),
        cost_estimate=cost(20 * gradient.size, 12 * gradient.size),
        name="prepare",
    )(slot_block, gradient, first_moment, second_moment)


def unpack_kernel(got_ref, ring_ref, adam_ref):
    count, order = ring_ref.shape[:2]
    rows = order // got_ref.shape[0]
    for i in range(count):
        ring_ref[i] = got_ref[:, i * rows : (i + 1) * rows, :].reshape(order, 128)
    at = count * rows
    total = got_ref[0, at:, :].astype(F32)
    for d in range(1, got_ref.shape[0]):
        total = total + got_ref[d, at:, :].astype(F32)
    adam_ref[...] = total


def unpack(count, got):
    order = (got.shape[1] - PAD) // count * got.shape[0]
    shape = (count, order, 128)
    return pl.pallas_call(
        unpack_kernel,
        out_shape=[
            jax.ShapeDtypeStruct(shape, BF16),
            jax.ShapeDtypeStruct((PAD, 128), F32),
        ],
        grid=(1,),
        in_specs=[whole(got.shape)],
        out_specs=[whole(shape), whole((PAD, 128))],
        compiler_params=params(16),
        cost_estimate=cost(0, 4 * got.size),
        name="unpack",
    )(got)


class RingPanels:
    def __init__(self, place, refs):
        self.place = place
        self.refs = refs

    def place_of(self, k):
        return lax.rem(self.place + k, 8)

    def rows(self, k, low, high):
        if k != 4:
            return self.refs[k if k < 4 else k + 1][low:high, :]
        upper, lower = self.refs[4:6]
        half = upper.shape[0]
        if high <= half:
            return upper[low:high, :]
        if low >= half:
            return lower[low - half : high - half, :]
        return jnp.concatenate([upper[low:, :], lower[: high - half, :]], axis=0)

    def rows_at(self, k, at):
        if k != 4:
            return self.refs[k if k < 4 else k + 1][pl.ds(at, 128), :]
        upper, lower = self.refs[4:6]
        half = upper.shape[0]
        inside = pl.ds(pl.multiple_of(lax.rem(at, half), 128), 128)
        return jnp.where(at < half, upper[inside, :], lower[inside, :])

    def mine(self):
        return self.refs[0][...]


def pair_of(grads, k, order):
    return jnp.concatenate([grads.rows(2 * k + e, 0, order) for e in range(2)], axis=1)


def bulk_kernel(left_ref, *refs):
    grads, roots, out_ref = refs[:7], refs[7:14], refs[14]
    left = left_ref[...]
    half = []
    for k in (0, 2, 4, 6):
        pair = [ref[...] for ref in grads[k : k + 2]]
        pair = jnp.concatenate(pair, axis=1) if len(pair) > 1 else pair[0]
        half.append(jnp.dot(left, pair, preferred_element_type=F32).astype(BF16))
    half = jnp.concatenate(half, axis=1)
    for c in range(4):
        column = slice(256 * c, 256 * (c + 1))
        part = jnp.concatenate([ref[:, column] for ref in roots], axis=0)
        out_ref[:, column] = jnp.dot(half, part, preferred_element_type=F32)


def bulk(left_root, grads, roots):
    count, rows, order = left_root.shape
    early = [*grads[:4], *grads[6:], *roots[:4], *roots[6:]]
    return pl.pallas_call(
        bulk_kernel,
        out_shape=jax.ShapeDtypeStruct(left_root.shape, F32),
        grid=(count,),
        in_specs=[slot_of(left_root.shape)] + [slot_of(panel.shape) for panel in early],
        out_specs=slot_of(left_root.shape),
        compiler_params=params(62),
        cost_estimate=cost(count * 4 * rows * order * order, count * 5 * order * order),
        name="bulk",
    )(left_root, *early)


def precondition_kernel(place_ref, left_ref, adam_ref, part_ref, *refs):
    out_refs, sums_ref = refs[4:12], refs[12]
    count = pl.num_programs(0)
    step = pl.program_id(0)
    rows = pl.ds(pl.multiple_of(step * 128, 128), 128)
    panel = jnp.concatenate([refs[0][...], refs[1][...]], axis=0)
    half = jnp.dot(left_ref[...], panel, preferred_element_type=F32).astype(BF16)
    square = jnp.zeros((1, 128), F32)
    largest = jnp.zeros((1, 128), F32)
    for k in range(8):
        column = pl.ds(pl.multiple_of(lax.rem(place_ref[0] + k, 8) * 128, 128), 128)
        root = jnp.concatenate([refs[2][:, column], refs[3][:, column]], axis=0)
        pre = part_ref[:, column] + jnp.dot(half, root, preferred_element_type=F32)
        out_refs[k][rows, :] = pre.astype(BF16)
        square = square + jnp.sum(pre * pre, axis=0, keepdims=True)
        largest = jnp.maximum(largest, jnp.max(jnp.abs(pre), axis=0, keepdims=True))
    low = 3 * step
    row = lax.broadcasted_iota(jnp.int32, (PAD, 128), 0)
    inside = (row >= low) & (row < low + 3)
    adam = jnp.sum(jnp.where(inside, adam_ref[...], 0.0), axis=0, keepdims=True)
    lane = lax.broadcasted_iota(jnp.int32, (1, 128), 1)

    @pl.when(step == 0)
    def _():
        sums_ref[...] = jnp.zeros((1, 128), F32)

    sums = sums_ref[...]
    for at, value in (
        (step, jnp.sum(adam, axis=1, keepdims=True)),
        (count + step, jnp.sum(square, axis=1, keepdims=True)),
        (2 * count + step, jnp.max(largest, axis=1, keepdims=True)),
    ):
        sums = jnp.where(lane == at, jnp.broadcast_to(value, (1, 128)), sums)
    sums_ref[...] = sums

    @pl.when(step == count - 1)
    def _():
        tile = split_rows([sums])
        for out_ref in out_refs:
            out_ref[out_ref.shape[0] - PAD :, :] = tile


def precondition(place, left_root, adam, part, grads, roots):
    count, rows, order = left_root.shape
    out = (count * rows + PAD, 128)
    late = [*grads[4:6], *roots[4:6]]
    return pl.pallas_call(
        precondition_kernel,
        out_shape=[jax.ShapeDtypeStruct(out, BF16)] * 8,
        grid=(count,),
        in_specs=[scalars(), slot_of(left_root.shape), whole(adam.shape), slot_of(part.shape)]
        + [slot_of(panel.shape) for panel in late],
        out_specs=[whole(out)] * 8,
        scratch_shapes=[pltpu.VMEM((1, 128), F32)],
        compiler_params=params(16),
        cost_estimate=cost(count * 4 * rows * 128 * order, count * 4 * rows * order),
        name="precondition",
    )(place, left_root, adam, part, *late)


def scale_kernel(count, place_ref, *refs):
    got_refs, out_ref = refs[:-1], refs[-1]
    rows = (out_ref.shape[1] - PAD) // count
    each = 128 // rows
    lane = lax.broadcasted_iota(jnp.int32, (1, 128), 1)
    total = largest = jnp.zeros((1, 128), F32)
    for ref in got_refs:
        values = joined(ref[count * 128 :, :].astype(F32), 0)
        total = total + values
        largest = jnp.maximum(largest, values)

    def only(values, at):
        one = jnp.sum(jnp.where(lane == at, values, 0.0), axis=1, keepdims=True)
        return jnp.broadcast_to(one, (1, 128))

    scales = []
    peak = jnp.zeros((1, 128), F32)
    for i in range(count):
        adam, square = only(total, i), only(total, count + i)
        scale = jnp.sqrt(adam) / jnp.sqrt(square + NORM_EPS)
        scales.append(scale)
        peak = jnp.maximum(peak, scale * only(largest, 2 * count + i))
    tile = split_rows(scales + [peak])
    for k, ref in enumerate(got_refs):
        first = lax.rem(place_ref[0] + 8 - k, 8) * each
        for e in range(each):
            for i in range(count):
                low = i * 128 + e * rows
                out_ref[first + e, i * rows : (i + 1) * rows, :] = ref[low : low + rows, :]
            out_ref[first + e, count * rows :, :] = tile


def scale_up(owners, count, place, gots):
    out = (owners, count * (1024 // owners) + PAD, 128)
    return pl.pallas_call(
        functools.partial(scale_kernel, count),
        out_shape=jax.ShapeDtypeStruct(out, BF16),
        grid=(1,),
        in_specs=[scalars()] + [whole(got.shape) for got in gots],
        out_specs=whole(out),
        compiler_params=params(16),
        cost_estimate=cost(0, 32 * gots[0].size),
        name="scale",
    )(place, *gots)


def finish_kernel(count, slot_ref, got_ref, out_ref):
    rows = out_ref.shape[1]
    owners = got_ref.shape[0]

    def carried(owner, k):
        return joined(got_ref[owner, count * rows :, :].astype(F32), k)

    def find(owner, peak):
        return jnp.maximum(peak, carried(owner, count))

    peak = lax.fori_loop(0, owners, find, jnp.zeros((1, 128), F32))
    clip = jnp.minimum(1.0, CLIP_LIMIT / peak)

    def body(owner, _):
        for i in range(count):
            graft = got_ref[owner, i * rows : (i + 1) * rows, :].astype(F32) * carried(owner, i)
            out_ref[slot_ref[owner * count + i]] = (graft * clip).astype(BF16)
        return 0

    lax.fori_loop(0, owners, body, 0)


def finish(count, slot_block, got):
    out = (slot_block.shape[0], (got.shape[1] - PAD) // count, 128)
    return pl.pallas_call(
        functools.partial(finish_kernel, count),
        out_shape=jax.ShapeDtypeStruct(out, BF16),
        grid=(1,),
        in_specs=[scalars(), whole(got.shape)],
        out_specs=whole(out),
        compiler_params=params(16),
        cost_estimate=cost(0, 4 * got.size),
        name="finish",
    )(slot_block, got)


def factors_kernel(place_ref, left_ref, right_ref, *refs):
    left_out, right_out = refs[-2:]
    order = left_ref.shape[1]
    place = place_ref[0]
    grads = RingPanels(place, refs[:9])
    at = pl.multiple_of(place * 128, 128)
    mine = jnp.concatenate([grads.rows_at(k, at) for k in range(8)], axis=1)
    for c in range(4):
        low = 256 * c
        rows = jnp.concatenate([grads.rows(k, low, low + 256) for k in range(8)], axis=1)
        part = lax.dot_general(
            mine, rows, (((1,), (1,)), ((), ())), preferred_element_type=F32
        )
        old = left_ref[:, low : low + 256]
        left_out[:, low : low + 256] = STAT_DECAY * old + (1.0 - STAT_DECAY) * part
    turned = grads.mine().T
    for k in range(4):
        part = jnp.dot(turned, pair_of(grads, k, order), preferred_element_type=F32)
        for e in range(2):
            to = grads.place_of(2 * k + e) * 128
            column = pl.ds(to if isinstance(to, int) else pl.multiple_of(to, 128), 128)
            old = right_ref[:, column]
            new = STAT_DECAY * old + (1.0 - STAT_DECAY) * part[:, 128 * e : 128 * (e + 1)]
            right_out[:, column] = new


def factors(place, left_stat, right_stat, grads):
    count, _, order = left_stat.shape
    return pl.pallas_call(
        factors_kernel,
        out_shape=[jax.ShapeDtypeStruct(left_stat.shape, F32)] * 2,
        grid=(count,),
        in_specs=[scalars(), slot_of(left_stat.shape), slot_of(right_stat.shape)]
        + [slot_of(grad.shape) for grad in grads],
        out_specs=[slot_of(left_stat.shape)] * 2,
        compiler_params=params(62),
        cost_estimate=cost(count * 4 * 128 * order * order, count * 4 * order * order),
        name="factors",
    )(place, left_stat, right_stat, *grads)


def ring(own, axis):
    up = [(i, (i + 1) % 8) for i in range(8)]
    down = [(i, (i - 1) % 8) for i in range(8)]
    from_below, from_above = [own], [own]
    for _ in range(3):
        from_below.append(lax.ppermute(from_below[-1], "mp", up))
        from_above.append(lax.ppermute(from_above[-1], "mp", down))
    size = own.shape[axis]
    first = lax.slice_in_dim(from_below[3], 0, size // 2, axis=axis)
    second = lax.slice_in_dim(from_above[3], size // 2, size, axis=axis)
    first = lax.ppermute(first, "mp", up)
    second = lax.ppermute(second, "mp", down)
    return from_above + [first, second] + from_below[:0:-1]


def shards(
    gradient, slot_block, first_moment, second_moment, left_stat, right_stat, left_root, right_root
):
    count = left_stat.shape[0]
    owners = gradient.shape[0] // count
    place = lax.axis_index("mp").astype(jnp.int32).reshape(1)
    roots = ring(right_root, 1)
    sent = prepare(count, owners, slot_block, gradient, first_moment, second_moment)
    got = lax.all_to_all(sent, "dp", split_axis=0, concat_axis=0, tiled=True)
    own, adam = unpack(count, got)
    own, _ = lax.optimization_barrier((own, (roots[3], roots[6])))
    grads = ring(own, 1)
    part = bulk(left_root, grads, roots)
    sents = precondition(place, left_root, adam, part, grads, roots)
    gots = list(sents)
    for k in (4, 3, 5, 2, 6, 1, 7):
        gots[k] = lax.ppermute(sents[k], "mp", [(i, (i + k) % 8) for i in range(8)])
    sent = scale_up(owners, count, place, gots)
    got = lax.all_to_all(sent, "dp", split_axis=0, concat_axis=0, tiled=True)
    left_new, right_new = factors(place, left_stat, right_stat, grads)
    update = finish(count, slot_block, got)
    return (update, left_new, right_new)


def solution(mesh):
    return jax.shard_map(
        shards,
        mesh=mesh,
        in_specs=(
            P(None, "dp", "mp"),
            P(),
            P(None, "dp", "mp"),
            P(None, "dp", "mp"),
            P("dp", "mp", None),
            P("dp", "mp", None),
            P("dp", "mp", None),
            P("dp", "mp", None),
        ),
        out_specs=(P(None, "dp", "mp"), P("dp", "mp", None), P("dp", "mp", None)),
        check_vma=False,
    )
```

```python
import functools

import jax
import jax.numpy as jnp
from jax import lax
from jax.experimental import pallas as pl
from jax.experimental.pallas import tpu as pltpu
from jax.sharding import PartitionSpec as P

BETA_ONE = 0.9
BETA_TWO = 0.999
ADAM_EPS = 1e-08
STAT_DECAY = 0.9
CLIP_LIMIT = 1.0
NORM_EPS = 1e-06
PAD = 16
F32 = jnp.float32
BF16 = jnp.bfloat16
SMEM = pltpu.SMEM


def params(mib):
    return pltpu.CompilerParams(vmem_limit_bytes=mib * 1024 * 1024)


def scalars():
    return pl.BlockSpec(memory_space=SMEM)


def whole(shape):
    return pl.BlockSpec(tuple(shape), lambda g: (0,) * len(shape))


def slot_of(shape):
    return pl.BlockSpec((None,) + tuple(shape[1:]), lambda g: (g,) + (0,) * (len(shape) - 1))


def cost(flops, nbytes):
    return pl.CostEstimate(flops=int(flops), bytes_accessed=int(nbytes), transcendentals=0)


def split_rows(values):
    row = lax.broadcasted_iota(jnp.int32, (PAD, 128), 0)
    tile = jnp.zeros((PAD, 128), F32)
    for k, value in enumerate(values):
        high = value.astype(BF16).astype(F32)
        rest = value - high
        middle = rest.astype(BF16).astype(F32)
        low = rest - middle
        for at, piece in enumerate((high, middle, low)):
            tile = jnp.where(row == 3 * k + at, jnp.broadcast_to(piece, (PAD, 128)), tile)
    return tile.astype(BF16)


def joined(tile, k):
    return tile[3 * k : 3 * k + 1] + tile[3 * k + 1 : 3 * k + 2] + tile[3 * k + 2 : 3 * k + 3]


def prepare_kernel(count, slot_ref, grad_ref, one_ref, two_ref, out_ref):
    rows = grad_ref.shape[1]

    def body(owner, _):
        parts = []
        for i in range(count):
            block = slot_ref[owner * count + i]
            grad = grad_ref[block]
            out_ref[owner, i * rows : (i + 1) * rows, :] = grad
            wide = grad.astype(F32)
            moment_one = BETA_ONE * one_ref[block] + (1.0 - BETA_ONE) * wide
            moment_two = BETA_TWO * two_ref[block] + (1.0 - BETA_TWO) * wide * wide
            adam = moment_one / (jnp.sqrt(moment_two) + ADAM_EPS)
            parts.append(jnp.sum(adam * adam, axis=0, keepdims=True))
        out_ref[owner, count * rows :, :] = split_rows(parts)
        return 0

    lax.fori_loop(0, out_ref.shape[0], body, 0)


def prepare(count, owners, slot_block, gradient, first_moment, second_moment):
    rows = gradient.shape[1]
    return pl.pallas_call(
        functools.partial(prepare_kernel, count),
        out_shape=jax.ShapeDtypeStruct((owners, count * rows + PAD, 128), BF16),
        grid=(1,),
        in_specs=[scalars()] + [whole(gradient.shape)] * 3,
        out_specs=whole((owners, count * rows + PAD, 128)),
        compiler_params=params(62),
        cost_estimate=cost(20 * gradient.size, 12 * gradient.size),
        name="prepare",
    )(slot_block, gradient, first_moment, second_moment)


def unpack_kernel(got_ref, ring_ref, adam_ref):
    count, order = ring_ref.shape[:2]
    rows = order // got_ref.shape[0]
    for i in range(count):
        ring_ref[i] = got_ref[:, i * rows : (i + 1) * rows, :].reshape(order, 128)
    at = count * rows
    total = got_ref[0, at:, :].astype(F32)
    for d in range(1, got_ref.shape[0]):
        total = total + got_ref[d, at:, :].astype(F32)
    adam_ref[...] = total


def unpack(count, got):
    order = (got.shape[1] - PAD) // count * got.shape[0]
    shape = (count, order, 128)
    return pl.pallas_call(
        unpack_kernel,
        out_shape=[
            jax.ShapeDtypeStruct(shape, BF16),
            jax.ShapeDtypeStruct((PAD, 128), F32),
        ],
        grid=(1,),
        in_specs=[whole(got.shape)],
        out_specs=[whole(shape), whole((PAD, 128))],
        compiler_params=params(16),
        cost_estimate=cost(0, 4 * got.size),
        name="unpack",
    )(got)


class RingPanels:
    def __init__(self, place, refs):
        self.place = place
        self.refs = refs

    def place_of(self, k):
        return lax.rem(self.place + k, 8)

    def rows(self, k, low, high):
        if k != 4:
            return self.refs[k if k < 4 else k + 1][low:high, :]
        upper, lower = self.refs[4:6]
        half = upper.shape[0]
        if high <= half:
            return upper[low:high, :]
        if low >= half:
            return lower[low - half : high - half, :]
        return jnp.concatenate([upper[low:, :], lower[: high - half, :]], axis=0)

    def rows_at(self, k, at):
        if k != 4:
            return self.refs[k if k < 4 else k + 1][pl.ds(at, 128), :]
        upper, lower = self.refs[4:6]
        half = upper.shape[0]
        inside = pl.ds(pl.multiple_of(lax.rem(at, half), 128), 128)
        return jnp.where(at < half, upper[inside, :], lower[inside, :])

    def mine(self):
        return self.refs[0][...]


def pair_of(grads, k, order):
    return jnp.concatenate([grads.rows(2 * k + e, 0, order) for e in range(2)], axis=1)


def bulk_kernel(left_ref, *refs):
    grads, roots, out_ref = refs[:7], refs[7:14], refs[14]
    left = left_ref[...]
    half = []
    for k in (0, 2, 4, 6):
        pair = [ref[...] for ref in grads[k : k + 2]]
        pair = jnp.concatenate(pair, axis=1) if len(pair) > 1 else pair[0]
        half.append(jnp.dot(left, pair, preferred_element_type=F32).astype(BF16))
    half = jnp.concatenate(half, axis=1)
    for c in range(4):
        column = slice(256 * c, 256 * (c + 1))
        part = jnp.concatenate([ref[:, column] for ref in roots], axis=0)
        out_ref[:, column] = jnp.dot(half, part, preferred_element_type=F32)


def bulk(left_root, grads, roots):
    count, rows, order = left_root.shape
    early = [*grads[:4], *grads[6:], *roots[:4], *roots[6:]]
    return pl.pallas_call(
        bulk_kernel,
        out_shape=jax.ShapeDtypeStruct(left_root.shape, F32),
        grid=(count,),
        in_specs=[slot_of(left_root.shape)] + [slot_of(panel.shape) for panel in early],
        out_specs=slot_of(left_root.shape),
        compiler_params=params(56),
        cost_estimate=cost(count * 4 * rows * order * order, count * 5 * order * order),
        name="bulk",
    )(left_root, *early)


def precondition_kernel(place_ref, left_ref, adam_ref, part_ref, *refs):
    out_refs, sums_ref = refs[4:12], refs[12]
    count = pl.num_programs(0)
    step = pl.program_id(0)
    rows = pl.ds(pl.multiple_of(step * 128, 128), 128)
    panel = jnp.concatenate([refs[0][...], refs[1][...]], axis=0)
    half = jnp.dot(left_ref[...], panel, preferred_element_type=F32).astype(BF16)
    square = jnp.zeros((1, 128), F32)
    largest = jnp.zeros((1, 128), F32)
    for k in range(8):
        column = pl.ds(pl.multiple_of(lax.rem(place_ref[0] + k, 8) * 128, 128), 128)
        root = jnp.concatenate([refs[2][:, column], refs[3][:, column]], axis=0)
        pre = part_ref[:, column] + jnp.dot(half, root, preferred_element_type=F32)
        out_refs[k][rows, :] = pre.astype(BF16)
        square = square + jnp.sum(pre * pre, axis=0, keepdims=True)
        largest = jnp.maximum(largest, jnp.max(jnp.abs(pre), axis=0, keepdims=True))
    low = 3 * step
    row = lax.broadcasted_iota(jnp.int32, (PAD, 128), 0)
    inside = (row >= low) & (row < low + 3)
    adam = jnp.sum(jnp.where(inside, adam_ref[...], 0.0), axis=0, keepdims=True)
    lane = lax.broadcasted_iota(jnp.int32, (1, 128), 1)

    @pl.when(step == 0)
    def _():
        sums_ref[...] = jnp.zeros((1, 128), F32)

    sums = sums_ref[...]
    for at, value in (
        (step, jnp.sum(adam, axis=1, keepdims=True)),
        (count + step, jnp.sum(square, axis=1, keepdims=True)),
        (2 * count + step, jnp.max(largest, axis=1, keepdims=True)),
    ):
        sums = jnp.where(lane == at, jnp.broadcast_to(value, (1, 128)), sums)
    sums_ref[...] = sums

    @pl.when(step == count - 1)
    def _():
        tile = split_rows([sums])
        for out_ref in out_refs:
            out_ref[out_ref.shape[0] - PAD :, :] = tile


def precondition(place, left_root, adam, part, grads, roots):
    count, rows, order = left_root.shape
    out = (count * rows + PAD, 128)
    late = [*grads[4:6], *roots[4:6]]
    return pl.pallas_call(
        precondition_kernel,
        out_shape=[jax.ShapeDtypeStruct(out, BF16)] * 8,
        grid=(count,),
        in_specs=[scalars(), slot_of(left_root.shape), whole(adam.shape), slot_of(part.shape)]
        + [slot_of(panel.shape) for panel in late],
        out_specs=[whole(out)] * 8,
        scratch_shapes=[pltpu.VMEM((1, 128), F32)],
        compiler_params=params(16),
        cost_estimate=cost(count * 4 * rows * 128 * order, count * 4 * rows * order),
        name="precondition",
    )(place, left_root, adam, part, *late)


def scale_kernel(count, place_ref, *refs):
    got_refs, out_ref = refs[:-1], refs[-1]
    rows = (out_ref.shape[1] - PAD) // count
    each = 128 // rows
    lane = lax.broadcasted_iota(jnp.int32, (1, 128), 1)
    total = largest = jnp.zeros((1, 128), F32)
    for ref in got_refs:
        values = joined(ref[count * 128 :, :].astype(F32), 0)
        total = total + values
        largest = jnp.maximum(largest, values)

    def only(values, at):
        one = jnp.sum(jnp.where(lane == at, values, 0.0), axis=1, keepdims=True)
        return jnp.broadcast_to(one, (1, 128))

    scales = []
    peak = jnp.zeros((1, 128), F32)
    for i in range(count):
        adam, square = only(total, i), only(total, count + i)
        scale = jnp.sqrt(adam) / jnp.sqrt(square + NORM_EPS)
        scales.append(scale)
        peak = jnp.maximum(peak, scale * only(largest, 2 * count + i))
    tile = split_rows(scales + [peak])
    for k, ref in enumerate(got_refs):
        first = lax.rem(place_ref[0] + 8 - k, 8) * each
        for e in range(each):
            for i in range(count):
                low = i * 128 + e * rows
                out_ref[first + e, i * rows : (i + 1) * rows, :] = ref[low : low + rows, :]
            out_ref[first + e, count * rows :, :] = tile


def scale_up(owners, count, place, gots):
    out = (owners, count * (1024 // owners) + PAD, 128)
    return pl.pallas_call(
        functools.partial(scale_kernel, count),
        out_shape=jax.ShapeDtypeStruct(out, BF16),
        grid=(1,),
        in_specs=[scalars()] + [whole(got.shape) for got in gots],
        out_specs=whole(out),
        compiler_params=params(16),
        cost_estimate=cost(0, 32 * gots[0].size),
        name="scale",
    )(place, *gots)


def finish_kernel(count, slot_ref, got_ref, out_ref):
    rows = out_ref.shape[1]
    owners = got_ref.shape[0]

    def carried(owner, k):
        return joined(got_ref[owner, count * rows :, :].astype(F32), k)

    def find(owner, peak):
        return jnp.maximum(peak, carried(owner, count))

    peak = lax.fori_loop(0, owners, find, jnp.zeros((1, 128), F32))
    clip = jnp.minimum(1.0, CLIP_LIMIT / peak)

    def body(owner, _):
        for i in range(count):
            graft = got_ref[owner, i * rows : (i + 1) * rows, :].astype(F32) * carried(owner, i)
            out_ref[slot_ref[owner * count + i]] = (graft * clip).astype(BF16)
        return 0

    lax.fori_loop(0, owners, body, 0)


def finish(count, slot_block, got):
    out = (slot_block.shape[0], (got.shape[1] - PAD) // count, 128)
    return pl.pallas_call(
        functools.partial(finish_kernel, count),
        out_shape=jax.ShapeDtypeStruct(out, BF16),
        grid=(1,),
        in_specs=[scalars(), whole(got.shape)],
        out_specs=whole(out),
        compiler_params=params(16),
        cost_estimate=cost(0, 4 * got.size),
        name="finish",
    )(slot_block, got)


def factors_kernel(place_ref, left_ref, right_ref, *refs):
    left_out, right_out = refs[-2:]
    order = left_ref.shape[1]
    place = place_ref[0]
    grads = RingPanels(place, refs[:9])
    at = pl.multiple_of(place * 128, 128)
    mine = jnp.concatenate([grads.rows_at(k, at) for k in range(8)], axis=1)
    for c in range(4):
        low = 256 * c
        rows = jnp.concatenate([grads.rows(k, low, low + 256) for k in range(8)], axis=1)
        part = lax.dot_general(
            mine, rows, (((1,), (1,)), ((), ())), preferred_element_type=F32
        )
        old = left_ref[:, low : low + 256]
        left_out[:, low : low + 256] = STAT_DECAY * old + (1.0 - STAT_DECAY) * part
    turned = grads.mine().T
    for k in range(4):
        part = jnp.dot(turned, pair_of(grads, k, order), preferred_element_type=F32)
        for e in range(2):
            to = grads.place_of(2 * k + e) * 128
            column = pl.ds(to if isinstance(to, int) else pl.multiple_of(to, 128), 128)
            old = right_ref[:, column]
            new = STAT_DECAY * old + (1.0 - STAT_DECAY) * part[:, 128 * e : 128 * (e + 1)]
            right_out[:, column] = new


def factors(place, left_stat, right_stat, grads):
    count, _, order = left_stat.shape
    return pl.pallas_call(
        factors_kernel,
        out_shape=[jax.ShapeDtypeStruct(left_stat.shape, F32)] * 2,
        grid=(count,),
        in_specs=[scalars(), slot_of(left_stat.shape), slot_of(right_stat.shape)]
        + [slot_of(grad.shape) for grad in grads],
        out_specs=[slot_of(left_stat.shape)] * 2,
        compiler_params=params(62),
        cost_estimate=cost(count * 4 * 128 * order * order, count * 4 * order * order),
        name="factors",
    )(place, left_stat, right_stat, *grads)


def ring(own, axis):
    up = [(i, (i + 1) % 8) for i in range(8)]
    down = [(i, (i - 1) % 8) for i in range(8)]
    from_below, from_above = [own], [own]
    for _ in range(3):
        from_below.append(lax.ppermute(from_below[-1], "mp", up))
        from_above.append(lax.ppermute(from_above[-1], "mp", down))
    size = own.shape[axis]
    first = lax.slice_in_dim(from_below[3], 0, size // 2, axis=axis)
    second = lax.slice_in_dim(from_above[3], size // 2, size, axis=axis)
    first = lax.ppermute(first, "mp", up)
    second = lax.ppermute(second, "mp", down)
    return from_above + [first, second] + from_below[:0:-1]


def shards(
    gradient, slot_block, first_moment, second_moment, left_stat, right_stat, left_root, right_root
):
    count = left_stat.shape[0]
    owners = gradient.shape[0] // count
    place = lax.axis_index("mp").astype(jnp.int32).reshape(1)
    roots = ring(right_root, 1)
    sent = prepare(count, owners, slot_block, gradient, first_moment, second_moment)
    got = lax.all_to_all(sent, "dp", split_axis=0, concat_axis=0, tiled=True)
    own, adam = unpack(count, got)
    own, _ = lax.optimization_barrier((own, (roots[3], roots[6])))
    grads = ring(own, 1)
    part = bulk(left_root, grads, roots)
    sents = precondition(place, left_root, adam, part, grads, roots)
    gots = list(sents)
    for k in (3, 5, 4, 2, 6, 1, 7):
        gots[k] = lax.ppermute(sents[k], "mp", [(i, (i + k) % 8) for i in range(8)])
    sent = scale_up(owners, count, place, gots)
    got = lax.all_to_all(sent, "dp", split_axis=0, concat_axis=0, tiled=True)
    left_new, right_new = factors(place, left_stat, right_stat, grads)
    update = finish(count, slot_block, got)
    return (update, left_new, right_new)


def solution(mesh):
    return jax.shard_map(
        shards,
        mesh=mesh,
        in_specs=(
            P(None, "dp", "mp"),
            P(),
            P(None, "dp", "mp"),
            P(None, "dp", "mp"),
            P("dp", "mp", None),
            P("dp", "mp", None),
            P("dp", "mp", None),
            P("dp", "mp", None),
        ),
        out_specs=(P(None, "dp", "mp"), P("dp", "mp", None), P("dp", "mp", None)),
        check_vma=False,
    )
```

```python
import functools

import jax
import jax.numpy as jnp
from jax import lax
from jax.experimental import pallas as pl
from jax.experimental.pallas import tpu as pltpu
from jax.sharding import PartitionSpec as P

BETA_ONE = 0.9
BETA_TWO = 0.999
ADAM_EPS = 1e-08
STAT_DECAY = 0.9
CLIP_LIMIT = 1.0
NORM_EPS = 1e-06
PAD = 16
F32 = jnp.float32
BF16 = jnp.bfloat16
SMEM = pltpu.SMEM


def params(mib):
    return pltpu.CompilerParams(vmem_limit_bytes=mib * 1024 * 1024)


def scalars():
    return pl.BlockSpec(memory_space=SMEM)


def whole(shape):
    return pl.BlockSpec(tuple(shape), lambda g: (0,) * len(shape))


def slot_of(shape):
    return pl.BlockSpec((None,) + tuple(shape[1:]), lambda g: (g,) + (0,) * (len(shape) - 1))


def cost(flops, nbytes):
    return pl.CostEstimate(flops=int(flops), bytes_accessed=int(nbytes), transcendentals=0)


def split_rows(values):
    row = lax.broadcasted_iota(jnp.int32, (PAD, 128), 0)
    tile = jnp.zeros((PAD, 128), F32)
    for k, value in enumerate(values):
        high = value.astype(BF16).astype(F32)
        rest = value - high
        middle = rest.astype(BF16).astype(F32)
        low = rest - middle
        for at, piece in enumerate((high, middle, low)):
            tile = jnp.where(row == 3 * k + at, jnp.broadcast_to(piece, (PAD, 128)), tile)
    return tile.astype(BF16)


def joined(tile, k):
    return tile[3 * k : 3 * k + 1] + tile[3 * k + 1 : 3 * k + 2] + tile[3 * k + 2 : 3 * k + 3]


def prepare_kernel(count, slot_ref, grad_ref, one_ref, two_ref, out_ref):
    rows = grad_ref.shape[1]

    def body(owner, _):
        parts = []
        for i in range(count):
            block = slot_ref[owner * count + i]
            grad = grad_ref[block]
            out_ref[owner, i * rows : (i + 1) * rows, :] = grad
            wide = grad.astype(F32)
            moment_one = BETA_ONE * one_ref[block] + (1.0 - BETA_ONE) * wide
            moment_two = BETA_TWO * two_ref[block] + (1.0 - BETA_TWO) * wide * wide
            adam = moment_one / (jnp.sqrt(moment_two) + ADAM_EPS)
            parts.append(jnp.sum(adam * adam, axis=0, keepdims=True))
        out_ref[owner, count * rows :, :] = split_rows(parts)
        return 0

    lax.fori_loop(0, out_ref.shape[0], body, 0)


def prepare(count, owners, slot_block, gradient, first_moment, second_moment):
    rows = gradient.shape[1]
    return pl.pallas_call(
        functools.partial(prepare_kernel, count),
        out_shape=jax.ShapeDtypeStruct((owners, count * rows + PAD, 128), BF16),
        grid=(1,),
        in_specs=[scalars()] + [whole(gradient.shape)] * 3,
        out_specs=whole((owners, count * rows + PAD, 128)),
        compiler_params=params(62),
        cost_estimate=cost(20 * gradient.size, 12 * gradient.size),
        name="prepare",
    )(slot_block, gradient, first_moment, second_moment)


def unpack_kernel(got_ref, ring_ref, adam_ref):
    count, order = ring_ref.shape[:2]
    rows = order // got_ref.shape[0]
    for i in range(count):
        ring_ref[i] = got_ref[:, i * rows : (i + 1) * rows, :].reshape(order, 128)
    at = count * rows
    total = got_ref[0, at:, :].astype(F32)
    for d in range(1, got_ref.shape[0]):
        total = total + got_ref[d, at:, :].astype(F32)
    adam_ref[...] = total


def unpack(count, got):
    order = (got.shape[1] - PAD) // count * got.shape[0]
    shape = (count, order, 128)
    return pl.pallas_call(
        unpack_kernel,
        out_shape=[
            jax.ShapeDtypeStruct(shape, BF16),
            jax.ShapeDtypeStruct((PAD, 128), F32),
        ],
        grid=(1,),
        in_specs=[whole(got.shape)],
        out_specs=[whole(shape), whole((PAD, 128))],
        compiler_params=params(16),
        cost_estimate=cost(0, 4 * got.size),
        name="unpack",
    )(got)


class RingPanels:
    def __init__(self, place, refs):
        self.place = place
        self.refs = refs

    def place_of(self, k):
        return lax.rem(self.place + k, 8)

    def rows(self, k, low, high):
        if k != 4:
            return self.refs[k if k < 4 else k + 1][low:high, :]
        upper, lower = self.refs[4:6]
        half = upper.shape[0]
        if high <= half:
            return upper[low:high, :]
        if low >= half:
            return lower[low - half : high - half, :]
        return jnp.concatenate([upper[low:, :], lower[: high - half, :]], axis=0)

    def rows_at(self, k, at):
        if k != 4:
            return self.refs[k if k < 4 else k + 1][pl.ds(at, 128), :]
        upper, lower = self.refs[4:6]
        half = upper.shape[0]
        inside = pl.ds(pl.multiple_of(lax.rem(at, half), 128), 128)
        return jnp.where(at < half, upper[inside, :], lower[inside, :])

    def mine(self):
        return self.refs[0][...]


def pair_of(grads, k, order):
    return jnp.concatenate([grads.rows(2 * k + e, 0, order) for e in range(2)], axis=1)


def bulk_kernel(left_ref, *refs):
    grads, roots, out_ref = refs[:7], refs[7:14], refs[14]
    left = left_ref[...]
    half = []
    for k in (0, 2, 4, 6):
        pair = [ref[...] for ref in grads[k : k + 2]]
        pair = jnp.concatenate(pair, axis=1) if len(pair) > 1 else pair[0]
        half.append(jnp.dot(left, pair, preferred_element_type=F32).astype(BF16))
    half = jnp.concatenate(half, axis=1)
    for c in range(4):
        column = slice(256 * c, 256 * (c + 1))
        part = jnp.concatenate([ref[:, column] for ref in roots], axis=0)
        out_ref[:, column] = jnp.dot(half, part, preferred_element_type=F32)


def bulk(left_root, grads, roots):
    count, rows, order = left_root.shape
    early = [*grads[:4], *grads[6:], *roots[:4], *roots[6:]]
    return pl.pallas_call(
        bulk_kernel,
        out_shape=jax.ShapeDtypeStruct(left_root.shape, F32),
        grid=(count,),
        in_specs=[slot_of(left_root.shape)] + [slot_of(panel.shape) for panel in early],
        out_specs=slot_of(left_root.shape),
        compiler_params=params(56),
        cost_estimate=cost(count * 4 * rows * order * order, count * 5 * order * order),
        name="bulk",
    )(left_root, *early)


def precondition_kernel(place_ref, left_ref, adam_ref, part_ref, *refs):
    out_refs, sums_ref, near_ref, arrived = refs[4:12], refs[12], refs[13], refs[14]
    count = pl.num_programs(0)
    step = pl.program_id(0)

    def fetch(slot):
        return pltpu.make_async_copy(part_ref.at[slot], near_ref.at[slot], arrived.at[slot])

    @pl.when(step == 0)
    def _():
        for slot in range(part_ref.shape[0]):
            fetch(slot).start()

    rows = pl.ds(pl.multiple_of(step * 128, 128), 128)
    panel = jnp.concatenate([refs[0][...], refs[1][...]], axis=0)
    half = jnp.dot(left_ref[...], panel, preferred_element_type=F32).astype(BF16)
    fetch(step).wait()
    square = jnp.zeros((1, 128), F32)
    largest = jnp.zeros((1, 128), F32)
    for k in range(8):
        column = pl.ds(pl.multiple_of(lax.rem(place_ref[0] + k, 8) * 128, 128), 128)
        root = jnp.concatenate([refs[2][:, column], refs[3][:, column]], axis=0)
        pre = near_ref[step, :, column] + jnp.dot(half, root, preferred_element_type=F32)
        out_refs[k][rows, :] = pre.astype(BF16)
        square = square + jnp.sum(pre * pre, axis=0, keepdims=True)
        largest = jnp.maximum(largest, jnp.max(jnp.abs(pre), axis=0, keepdims=True))
    low = 3 * step
    row = lax.broadcasted_iota(jnp.int32, (PAD, 128), 0)
    inside = (row >= low) & (row < low + 3)
    adam = jnp.sum(jnp.where(inside, adam_ref[...], 0.0), axis=0, keepdims=True)
    lane = lax.broadcasted_iota(jnp.int32, (1, 128), 1)

    @pl.when(step == 0)
    def _():
        sums_ref[...] = jnp.zeros((1, 128), F32)

    sums = sums_ref[...]
    for at, value in (
        (step, jnp.sum(adam, axis=1, keepdims=True)),
        (count + step, jnp.sum(square, axis=1, keepdims=True)),
        (2 * count + step, jnp.max(largest, axis=1, keepdims=True)),
    ):
        sums = jnp.where(lane == at, jnp.broadcast_to(value, (1, 128)), sums)
    sums_ref[...] = sums

    @pl.when(step == count - 1)
    def _():
        tile = split_rows([sums])
        for out_ref in out_refs:
            out_ref[out_ref.shape[0] - PAD :, :] = tile


def precondition(place, left_root, adam, part, grads, roots):
    count, rows, order = left_root.shape
    out = (count * rows + PAD, 128)
    late = [*grads[4:6], *roots[4:6]]
    return pl.pallas_call(
        precondition_kernel,
        out_shape=[jax.ShapeDtypeStruct(out, BF16)] * 8,
        grid=(count,),
        in_specs=[scalars(), slot_of(left_root.shape), whole(adam.shape)]
        + [pl.BlockSpec(memory_space=pltpu.HBM)]
        + [slot_of(panel.shape) for panel in late],
        out_specs=[whole(out)] * 8,
        scratch_shapes=[
            pltpu.VMEM((1, 128), F32),
            pltpu.VMEM(part.shape, F32),
            pltpu.SemaphoreType.DMA((count,)),
        ],
        compiler_params=params(60),
        cost_estimate=cost(count * 4 * rows * 128 * order, count * 4 * rows * order),
        name="precondition",
    )(place, left_root, adam, part, *late)


def scale_kernel(count, place_ref, *refs):
    got_refs, out_ref = refs[:-1], refs[-1]
    rows = (out_ref.shape[1] - PAD) // count
    each = 128 // rows
    lane = lax.broadcasted_iota(jnp.int32, (1, 128), 1)
    total = largest = jnp.zeros((1, 128), F32)
    for ref in got_refs:
        values = joined(ref[count * 128 :, :].astype(F32), 0)
        total = total + values
        largest = jnp.maximum(largest, values)

    def only(values, at):
        one = jnp.sum(jnp.where(lane == at, values, 0.0), axis=1, keepdims=True)
        return jnp.broadcast_to(one, (1, 128))

    scales = []
    peak = jnp.zeros((1, 128), F32)
    for i in range(count):
        adam, square = only(total, i), only(total, count + i)
        scale = jnp.sqrt(adam) / jnp.sqrt(square + NORM_EPS)
        scales.append(scale)
        peak = jnp.maximum(peak, scale * only(largest, 2 * count + i))
    tile = split_rows(scales + [peak])
    for k, ref in enumerate(got_refs):
        first = lax.rem(place_ref[0] + 8 - k, 8) * each
        for e in range(each):
            for i in range(count):
                low = i * 128 + e * rows
                out_ref[first + e, i * rows : (i + 1) * rows, :] = ref[low : low + rows, :]
            out_ref[first + e, count * rows :, :] = tile


def scale_up(owners, count, place, gots):
    out = (owners, count * (1024 // owners) + PAD, 128)
    return pl.pallas_call(
        functools.partial(scale_kernel, count),
        out_shape=jax.ShapeDtypeStruct(out, BF16),
        grid=(1,),
        in_specs=[scalars()] + [whole(got.shape) for got in gots],
        out_specs=whole(out),
        compiler_params=params(16),
        cost_estimate=cost(0, 32 * gots[0].size),
        name="scale",
    )(place, *gots)


def finish_kernel(count, slot_ref, got_ref, out_ref):
    rows = out_ref.shape[1]
    owners = got_ref.shape[0]

    def carried(owner, k):
        return joined(got_ref[owner, count * rows :, :].astype(F32), k)

    def find(owner, peak):
        return jnp.maximum(peak, carried(owner, count))

    peak = lax.fori_loop(0, owners, find, jnp.zeros((1, 128), F32))
    clip = jnp.minimum(1.0, CLIP_LIMIT / peak)

    def body(owner, _):
        for i in range(count):
            graft = got_ref[owner, i * rows : (i + 1) * rows, :].astype(F32) * carried(owner, i)
            out_ref[slot_ref[owner * count + i]] = (graft * clip).astype(BF16)
        return 0

    lax.fori_loop(0, owners, body, 0)


def finish(count, slot_block, got):
    out = (slot_block.shape[0], (got.shape[1] - PAD) // count, 128)
    return pl.pallas_call(
        functools.partial(finish_kernel, count),
        out_shape=jax.ShapeDtypeStruct(out, BF16),
        grid=(1,),
        in_specs=[scalars(), whole(got.shape)],
        out_specs=whole(out),
        compiler_params=params(16),
        cost_estimate=cost(0, 4 * got.size),
        name="finish",
    )(slot_block, got)


def factors_kernel(place_ref, left_ref, right_ref, *refs):
    left_out, right_out = refs[-2:]
    order = left_ref.shape[1]
    place = place_ref[0]
    grads = RingPanels(place, refs[:9])
    at = pl.multiple_of(place * 128, 128)
    mine = jnp.concatenate([grads.rows_at(k, at) for k in range(8)], axis=1)
    for c in range(4):
        low = 256 * c
        rows = jnp.concatenate([grads.rows(k, low, low + 256) for k in range(8)], axis=1)
        part = lax.dot_general(
            mine, rows, (((1,), (1,)), ((), ())), preferred_element_type=F32
        )
        old = left_ref[:, low : low + 256]
        left_out[:, low : low + 256] = STAT_DECAY * old + (1.0 - STAT_DECAY) * part
    turned = grads.mine().T
    for k in range(4):
        part = jnp.dot(turned, pair_of(grads, k, order), preferred_element_type=F32)
        for e in range(2):
            to = grads.place_of(2 * k + e) * 128
            column = pl.ds(to if isinstance(to, int) else pl.multiple_of(to, 128), 128)
            old = right_ref[:, column]
            new = STAT_DECAY * old + (1.0 - STAT_DECAY) * part[:, 128 * e : 128 * (e + 1)]
            right_out[:, column] = new


def factors(place, left_stat, right_stat, grads):
    count, _, order = left_stat.shape
    return pl.pallas_call(
        factors_kernel,
        out_shape=[jax.ShapeDtypeStruct(left_stat.shape, F32)] * 2,
        grid=(count,),
        in_specs=[scalars(), slot_of(left_stat.shape), slot_of(right_stat.shape)]
        + [slot_of(grad.shape) for grad in grads],
        out_specs=[slot_of(left_stat.shape)] * 2,
        compiler_params=params(62),
        cost_estimate=cost(count * 4 * 128 * order * order, count * 4 * order * order),
        name="factors",
    )(place, left_stat, right_stat, *grads)


def ring(own, axis):
    up = [(i, (i + 1) % 8) for i in range(8)]
    down = [(i, (i - 1) % 8) for i in range(8)]
    from_below, from_above = [own], [own]
    for _ in range(3):
        from_below.append(lax.ppermute(from_below[-1], "mp", up))
        from_above.append(lax.ppermute(from_above[-1], "mp", down))
    size = own.shape[axis]
    first = lax.slice_in_dim(from_below[3], 0, size // 2, axis=axis)
    second = lax.slice_in_dim(from_above[3], size // 2, size, axis=axis)
    first = lax.ppermute(first, "mp", up)
    second = lax.ppermute(second, "mp", down)
    return from_above + [first, second] + from_below[:0:-1]


def shards(
    gradient, slot_block, first_moment, second_moment, left_stat, right_stat, left_root, right_root
):
    count = left_stat.shape[0]
    owners = gradient.shape[0] // count
    place = lax.axis_index("mp").astype(jnp.int32).reshape(1)
    roots = ring(right_root, 1)
    sent = prepare(count, owners, slot_block, gradient, first_moment, second_moment)
    got = lax.all_to_all(sent, "dp", split_axis=0, concat_axis=0, tiled=True)
    own, adam = unpack(count, got)
    own, _ = lax.optimization_barrier((own, (roots[3], roots[6])))
    grads = ring(own, 1)
    part = bulk(left_root, grads, roots)
    sents = precondition(place, left_root, adam, part, grads, roots)
    gots = list(sents)
    for k in (3, 5, 4, 2, 6, 1, 7):
        gots[k] = lax.ppermute(sents[k], "mp", [(i, (i + k) % 8) for i in range(8)])
    sent = scale_up(owners, count, place, gots)
    got = lax.all_to_all(sent, "dp", split_axis=0, concat_axis=0, tiled=True)
    left_new, right_new = factors(place, left_stat, right_stat, grads)
    update = finish(count, slot_block, got)
    return (update, left_new, right_new)


def solution(mesh):
    return jax.shard_map(
        shards,
        mesh=mesh,
        in_specs=(
            P(None, "dp", "mp"),
            P(),
            P(None, "dp", "mp"),
            P(None, "dp", "mp"),
            P("dp", "mp", None),
            P("dp", "mp", None),
            P("dp", "mp", None),
            P("dp", "mp", None),
        ),
        out_specs=(P(None, "dp", "mp"), P("dp", "mp", None), P("dp", "mp", None)),
        check_vma=False,
    )
```
